32 devices in a mesh: prompts: 2 (over y), patch: 4 (over z), cfg: 2 (over core), batch: 2 (over x).
Axes of the slice: x: 2, y: 2, z: 4, core: 2. Of those that a mesh axis runs over, the one named last changes fastest.
Arguments:
- latent: float32 [4, 64, 1280], P(('prompts', 'batch'), 'patch'), parts along dimension 0, may hold values from -16 to 16
- stale_keys: bfloat16 [4, 64, 1280], P('prompts', 'patch', 'batch'), parts along dimension 0, may hold values from -18 to 18
- stale_values: bfloat16 [4, 64, 1280], P('prompts', 'patch', 'batch'), parts along dimension 0, may hold values from -12 to 12
- text_keys: bfloat16 [4, 77, 1280], P(('prompts', 'cfg'), None, 'batch'), parts along dimension 0, may hold values from -160 to 160
- text_values: bfloat16 [4, 77, 1280], P(('prompts', 'cfg'), None, 'batch'), parts along dimension 0, may hold values from -6 to 6
- w_query: bfloat16 [1280, 1280], P(None, 'batch'), may hold values from -0.15625 to 0.15625
- w_key: bfloat16 [1280, 1280], P(None, 'batch'), may hold values from -0.15625 to 0.15625
- w_value: bfloat16 [1280, 1280], P(None, 'batch'), may hold values from -0.15625 to 0.15625
- w_out: bfloat16 [1280, 1280], P('batch'), may hold values from -0.15625 to 0.15625
- norm_gain: float32 [1280], replicated, may hold values from 0.25 to 1.75
- norm_bias: float32 [1280], replicated, may hold values from -0.5 to 0.5
- timesteps: int32 [6], P('prompts'), parts along dimension 0, may hold values from 0 to 999, as said below
Outputs:
- final_latent: float32 [4, 64, 1280], P(('prompts', 'batch'), 'patch'), parts along dimension 0
- final_keys: bfloat16 [4, 64, 1280], P('prompts', 'patch', 'batch'), parts along dimension 0
- final_values: bfloat16 [4, 64, 1280], P('prompts', 'patch', 'batch'), parts along dimension 0
The draws below stay inside these ranges and needn't reach their ends.
There are 2 independent parts, one for each index of `prompts`. The reference program is written for one: setup_inputs(seed, part) draws one part's arguments, and reference() takes and returns one part's arrays. A program takes and returns all parts, laid end to end along the dimension named above; an argument that names none is the same for every part. Nothing has to cross between parts.
Inputs may be any that keep to these rules, and one draw needn't show every extreme that they name: `timesteps`: strictly falling from the first entry to the last.
All inputs are finite; a program needn't handle non-finite values.
Results may differ from the reference program's by a relative error of at most 0.035.
Values may be sent and summed in bfloat16 or wider, within the bound.
A program may use at most 64 MiB of HBM per device.

```python
import math
import jax
import jax.numpy as jnp
from jax import lax

D = 1280
HEADS = 20
HEAD = 64
GROUPS = 32
CTX = 77
STEPS = 2
TOK_DEV = 16
TOKENS = 64
IMAGES = 2
N_PATCH = 4


def draw_latent(key, part):
    base = jax.random.normal(key, (IMAGES, TOKENS, D), jnp.float32)
    place = jnp.arange(TOKENS, dtype=jnp.float32) / max(TOKENS - 1, 1)
    rising = 1.0 + 2.0 * place
    return jnp.clip(base * rising[None, :, None], -16.0, 16.0)


def draw_text_keys(key, part):
    base = jnp.clip(jax.random.normal(key, (2, CTX, D), jnp.float32), -4.0, 4.0)
    return base.astype(jnp.bfloat16)


def draw_timesteps(key, part):
    first = jax.random.randint(jax.random.fold_in(key, 1), (1,), 700, 1000)
    drops = jax.random.randint(jax.random.fold_in(key, 2), (STEPS,), 60, 301)
    falls = jnp.concatenate([jnp.zeros((1,), jnp.int32), jnp.cumsum(drops).astype(jnp.int32)])
    return (first.astype(jnp.int32) - falls).astype(jnp.int32)


def steps_of(own_key, dims, pieces, low, high):
    def one(position, blocks):
        steps = jax.random.uniform(jax.random.fold_in(jax.random.fold_in(own_key, 6), position), (blocks,), jnp.float32, low / len(pieces), high / len(pieces))
        return jnp.repeat(jnp.exp(steps), dims[position] // blocks).reshape((-1,) + (1,) * (len(dims) - position - 1))

    factor_of = one(*pieces[0])
    for cut in pieces[1:]:
        factor_of = factor_of * one(*cut)
    return factor_of


def gaussian(stream_key, extent, scale, reach, split=(), kind=jnp.bfloat16):
    factor_of = steps_of(stream_key, extent, split, -0.22, 0.18) if split else 1.0
    result = jax.random.normal(stream_key, extent, jnp.float32) * scale * factor_of
    return jnp.minimum(jnp.maximum(result, -reach), reach).astype(kind)


def setup_inputs(seed: int = 0, part: int = 0) -> dict:
    key_of = jax.random.split(jax.random.key(seed), 13)
    part_keys = jax.random.split(jax.random.fold_in(key_of[12], part), 13)
    return {
        "latent": draw_latent(jax.random.fold_in(jax.random.fold_in(key_of[12], part), 71), part),
        "stale_keys": gaussian(part_keys[1], (IMAGES, TOKENS, D), 3.0, 18.0, ((1, 4), (2, 2))),
        "stale_values": gaussian(part_keys[2], (IMAGES, TOKENS, D), 2.0, 12.0, ((1, 4), (2, 2))),
        "text_keys": draw_text_keys(jax.random.fold_in(jax.random.fold_in(key_of[12], part), 71), part),
        "text_values": gaussian(part_keys[4], (2, CTX, D), 1.0, 6.0, ((0, 2), (2, 2))),
        "w_query": gaussian(key_of[5], (D, D), D ** -0.5, 0.15625, ((1, 2),)),
        "w_key": gaussian(key_of[6], (D, D), D ** -0.5, 0.15625, ((1, 2),)),
        "w_value": gaussian(key_of[7], (D, D), D ** -0.5, 0.15625, ((1, 2),)),
        "w_out": gaussian(key_of[8], (D, D), D ** -0.5, 0.15625, ((0, 2),)),
        "norm_gain": jnp.clip(1.0 + 0.15 * jax.random.normal(key_of[9], (D,), jnp.float32), 0.25, 1.75),
        "norm_bias": jnp.clip(jax.random.uniform(key_of[10], (D,), jnp.float32, -0.5, 0.5), -0.5, 0.5),
        "timesteps": draw_timesteps(jax.random.fold_in(jax.random.fold_in(key_of[12], part), 71), part),
    }


guide_weight = 5.0
norm_eps = 1e-06

def alpha_bar(step_index):
    grid = jnp.arange(1000, dtype=jnp.int32)
    ramp = grid.astype(jnp.float32) / 999.0
    root = math.sqrt(0.00085) + ramp * (math.sqrt(0.012) - math.sqrt(0.00085))
    logs = jnp.cumsum(jnp.log1p(-root * root))
    picked = (grid == step_index).astype(jnp.float32)
    return jnp.exp(jnp.sum(picked * logs))

def sampler_weights(now, after):
    a_now = alpha_bar(now)
    a_next = alpha_bar(after)
    keep = jnp.sqrt(a_next / a_now)
    push = jnp.sqrt(1.0 - a_next) - keep * jnp.sqrt(1.0 - a_now)
    return (keep, push)

def group_norm(state, gain, bias):
    images, tokens, width = state.shape
    grouped = state.reshape(images, tokens, GROUPS, width // GROUPS)
    mean = lax.optimization_barrier(jnp.mean(grouped, axis=(1, 3), keepdims=True))
    square = lax.optimization_barrier(jnp.mean(grouped * grouped, axis=(1, 3), keepdims=True))
    scale = lax.rsqrt(square - mean * mean + norm_eps)
    normed = ((grouped - mean) * scale).reshape(images, tokens, width) * gain + bias
    return normed.astype(jnp.bfloat16)

def attend(queries, fresh_k, fresh_v, prior_k, prior_v, text_k, text_v):
    images, tokens, width = queries.shape
    text_kb = jnp.broadcast_to(text_k[None], (images,) + text_k.shape).astype(jnp.float32)
    text_vb = jnp.broadcast_to(text_v[None], (images,) + text_v.shape).astype(jnp.float32)

    def one_patch(patch):
        start = (patch * TOK_DEV).astype(jnp.int32)
        query = lax.dynamic_slice_in_dim(queries, start, TOK_DEV, 1).astype(jnp.float32)
        keys = lax.dynamic_update_slice_in_dim(prior_k, lax.dynamic_slice_in_dim(fresh_k, start, TOK_DEV, 1), start, 1)
        values = lax.dynamic_update_slice_in_dim(prior_v, lax.dynamic_slice_in_dim(fresh_v, start, TOK_DEV, 1), start, 1)
        keys = jnp.concatenate([keys.astype(jnp.float32), text_kb], axis=1)
        values = jnp.concatenate([values.astype(jnp.float32), text_vb], axis=1)
        query = query.reshape(images, TOK_DEV, HEADS, HEAD)
        keys = keys.reshape(images, keys.shape[1], HEADS, HEAD)
        values = values.reshape(images, values.shape[1], HEADS, HEAD)
        scores = jnp.einsum('bqhd,bkhd->bhqk', query, keys) * HEAD ** (-0.5)
        top = lax.optimization_barrier(jnp.max(scores, axis=-1, keepdims=True))
        weights = jnp.exp(scores - top)
        probs = (weights / lax.optimization_barrier(jnp.sum(weights, axis=-1, keepdims=True))).astype(jnp.bfloat16)
        out = jnp.einsum('bhqk,bkhd->bqhd', probs.astype(jnp.float32), values)
        return out.reshape(images, TOK_DEV, width).astype(jnp.bfloat16)
    blocks = lax.map(one_patch, jnp.arange(N_PATCH, dtype=jnp.int32))
    return jnp.transpose(blocks, (1, 0, 2, 3)).reshape(images, tokens, width)

def reference(latent, stale_keys, stale_values, text_keys, text_values, w_query, w_key, w_value, w_out, norm_gain, norm_bias, timesteps):
    state = latent
    images, tokens, width = latent.shape
    prior_k, prior_v = (stale_keys, stale_values)
    for step in range(STEPS):
        normed = group_norm(state, norm_gain, norm_bias)
        flat = normed.reshape(images * tokens, width)
        queries = jnp.dot(flat, w_query, preferred_element_type=jnp.float32).astype(jnp.bfloat16).reshape(images, tokens, width)
        fresh_k = jnp.dot(flat, w_key, preferred_element_type=jnp.float32).astype(jnp.bfloat16).reshape(images, tokens, width)
        fresh_v = jnp.dot(flat, w_value, preferred_element_type=jnp.float32).astype(jnp.bfloat16).reshape(images, tokens, width)
        branches = []
        for half in range(2):
            attended = attend(queries, fresh_k, fresh_v, prior_k, prior_v, text_keys[half], text_values[half])
            mixed = jnp.dot(attended.reshape(images * tokens, width), w_out, preferred_element_type=jnp.float32)
            branches.append(state + mixed.reshape(images, tokens, width))
        guess = branches[1] + guide_weight * (branches[0] - branches[1])
        keep, push = sampler_weights(timesteps[step], timesteps[step + 1])
        state = keep * state + push * guess
        prior_k, prior_v = (fresh_k, fresh_v)
    return (state, prior_k, prior_v)
```

```python
import functools
import math

import jax
import jax.numpy as jnp
from jax import lax
from jax.experimental import pallas as pl
from jax.experimental.pallas import tpu as pltpu
from jax.sharding import PartitionSpec as P

HEAD = 64
GROUPS = 32
STEPS = 2
LANES = 128

guide_weight = 5.0
norm_eps = 1e-06
MESH = pl.DeviceIdType.MESH
F32 = jnp.float32
BF16 = jnp.bfloat16


def split3(x):
    hi = x.astype(BF16)
    rest = x - hi.astype(F32)
    mid = rest.astype(BF16)
    low = (rest - mid.astype(F32)).astype(BF16)
    return hi, mid, low


def exact_dot(x, onehot, contract):
    rows = x.shape[0]
    parts = jnp.concatenate([p.astype(F32) for p in split3(x)], axis=0).astype(BF16)
    out = lax.dot_general(parts, onehot, (((1,), (contract,)), ((), ())), preferred_element_type=F32)
    return out[:rows] + out[rows : 2 * rows] + out[2 * rows :]


def kernel(
    n_patch,
    n_batch,
    latent,
    stale_k,
    stale_v,
    text_k,
    text_v,
    w_query,
    w_key,
    w_value,
    w_out,
    gain,
    bias,
    timesteps,
    out_state,
    out_k,
    out_v,
    state_v,
    tk_v,
    tv_v,
    wq_v,
    wk_v,
    wv_v,
    wo_v,
    k_all,
    v_all,
    fresh_kv,
    dev_send,
    dev_recv,
    cen_send,
    cen_recv,
    stat_send,
    stat_all,
    mix_send,
    mix_all,
    load_sem,
    kv_send_sem,
    kv_recv_sem,
    dev_send_sem,
    dev_recv_sem,
    stat_send_sem,
    stat_recv_sem,
    mix_send_sem,
    mix_recv_sem,
):
    patch = lax.axis_index("patch")
    half = lax.axis_index("cfg")
    batch = lax.axis_index("batch")
    tok = state_v.shape[0]
    width = state_v.shape[1]
    images = k_all.shape[2]
    local = wq_v.shape[1]
    heads = local // HEAD
    group_width = width // GROUPS
    count = float(tok * n_patch * group_width)

    loads = [
        pltpu.make_async_copy(src, dst, load_sem.at[i])
        for i, (src, dst) in enumerate(
            [
                (latent.at[0], state_v),
                (w_key, wk_v),
                (w_value, wv_v),
                (w_query, wq_v),
                (text_k.at[0], tk_v),
                (text_v.at[0], tv_v),
                (w_out, wo_v),
            ]
        )
    ]
    for copy in loads:
        copy.start()

    def peer(p, c, b):
        return {"patch": p, "cfg": c, "batch": b}

    others_pb = [(dp, db) for db in range(n_batch) for dp in range(n_patch) if (dp, db) != (0, 0)]
    others_bc = [(db, dc) for db in range(n_batch) for dc in range(2) if (db, dc) != (0, 0)]

    def at_patch(d):
        return lax.rem(patch + d, n_patch) if d else patch

    def at_batch(d):
        return lax.rem(batch + d, n_batch) if d else batch

    def at_half(d):
        return lax.rem(half + d, 2) if d else half

    barrier = pltpu.get_barrier_semaphore()
    greeted = 0
    for dp, db in others_pb:
        pl.semaphore_signal(barrier, inc=1, device_id=peer(at_patch(dp), half, at_batch(db)), device_id_type=MESH)
        greeted += 1
    for db, dc in others_bc:
        if dc:
            pl.semaphore_signal(barrier, inc=1, device_id=peer(patch, at_half(dc), at_batch(db)), device_id_type=MESH)
            greeted += 1

    chan = lax.broadcasted_iota(jnp.int32, (width, LANES), 0)
    lane = lax.broadcasted_iota(jnp.int32, (width, LANES), 1)
    low = lane * group_width
    onehot = jnp.where((chan >= low) & (chan < low + group_width), 1.0, 0.0).astype(BF16)

    head_id = lax.broadcasted_iota(jnp.int32, (heads, tok, local), 0) * HEAD
    col_id = lax.broadcasted_iota(jnp.int32, (heads, tok, local), 2)
    head_mask = (col_id >= head_id) & (col_id < head_id + HEAD)

    sub = lax.broadcasted_iota(jnp.int32, (8, LANES), 0)
    lan = lax.broadcasted_iota(jnp.int32, (8, LANES), 1)
    grid = sub * LANES + lan
    ramp = grid.astype(F32) / 999.0
    root = math.sqrt(0.00085) + ramp * (math.sqrt(0.012) - math.sqrt(0.00085))
    logs = jnp.log1p(-root * root)

    def alpha_bar(t):
        picked = jnp.where((grid <= t) & (grid < 1000), logs, 0.0)
        return jnp.exp(jnp.sum(jnp.sum(picked, axis=1, keepdims=True), axis=0, keepdims=True))

    abar = [alpha_bar(timesteps[0, s]) for s in range(STEPS + 1)]

    def send_kv(step, src_k, src_v):
        made = []
        for d in range(1, n_patch):
            for j, (src, dst) in enumerate([(src_k, k_all), (src_v, v_all)]):
                copy = pltpu.make_async_remote_copy(
                    src_ref=src,
                    dst_ref=dst.at[step, :, :, pl.ds(pl.multiple_of(patch * tok, tok), tok), :].at[0],
                    send_sem=kv_send_sem.at[step, j, d],
                    recv_sem=kv_recv_sem.at[step, j, d],
                    device_id=peer(at_patch(d), half, batch),
                    device_id_type=MESH,
                )
                copy.start()
                made.append(copy)
        return made

    sent = []
    loads[0].wait()
    state = state_v[...]
    gain_row = gain[...]
    bias_row = bias[...]

    for step in range(STEPS):
        col_sum = jnp.sum(state, axis=0, keepdims=True)
        col_sq = jnp.sum(state * state, axis=0, keepdims=True)
        centre = col_sum / float(tok)
        cen_send[step] = centre
        dev_send[step] = (state - centre).astype(BF16)
        if step == 0:
            pl.semaphore_wait(barrier, greeted)
        dev_waits = []
        for d in range(1, n_batch):
            for j, (src, dst) in enumerate([(dev_send, dev_recv), (cen_send, cen_recv)]):
                copy = pltpu.make_async_remote_copy(
                    src_ref=src.at[step],
                    dst_ref=dst.at[step, d],
                    send_sem=dev_send_sem.at[step, j, d],
                    recv_sem=dev_recv_sem.at[step, j, d],
                    device_id=peer(patch, half, at_batch(d)),
                    device_id_type=MESH,
                )
                copy.start()
                dev_waits.append(copy)
        pad = jnp.zeros((6, width), F32)
        compact = exact_dot(jnp.concatenate([col_sum, col_sq, pad], axis=0), onehot, 0)
        stat_send[step] = compact
        stat_all[step, batch, patch] = compact
        stat_waits = []
        for dp, db in others_pb:
            copy = pltpu.make_async_remote_copy(
                src_ref=stat_send.at[step],
                dst_ref=stat_all.at[step, batch, patch],
                send_sem=stat_send_sem.at[step, db, dp],
                recv_sem=stat_recv_sem.at[step, db, dp],
                device_id=peer(at_patch(dp), half, at_batch(db)),
                device_id_type=MESH,
            )
            copy.start()
            stat_waits.append(copy)
        if step == 0:
            sent += send_kv(0, stale_k, stale_v)
            kv_waits = sent[-2 * (n_patch - 1) :]
        for copy in stat_waits:
            copy.wait()

        rows = []
        for d in range(n_batch):
            total = stat_all[step, at_batch(d), 0]
            for p in range(1, n_patch):
                total = total + stat_all[step, at_batch(d), p]
            total = total / count
            mean = total[0:1]
            scale = lax.rsqrt(total[1:2] - mean * mean + norm_eps)
            rows += [mean, scale]
        pad_rows = -len(rows) % 8
        if pad_rows:
            rows.append(jnp.zeros((pad_rows, LANES), F32))
        wide = exact_dot(jnp.concatenate(rows, axis=0), onehot, 1)
        for copy in dev_waits:
            copy.wait()
        pieces = []
        for d in range(n_batch):
            mean = wide[2 * d : 2 * d + 1]
            scale = wide[2 * d + 1 : 2 * d + 2]
            if d == 0:
                shifted = state - mean
            else:
                shifted = dev_recv[step, n_batch - d].astype(F32) + (cen_recv[step, n_batch - d] - mean)
            pieces.append((shifted * scale * gain_row + bias_row).astype(BF16))
        normed = jnp.concatenate(pieces, axis=0)

        own = pl.ds(pl.multiple_of(patch * tok, tok), tok)
        if step == 0:
            loads[1].wait()
        keys = jnp.dot(normed, wk_v[...], preferred_element_type=F32).astype(BF16)
        for d in range(n_batch):
            block = keys[d * tok : (d + 1) * tok]
            k_all[step, 0, at_batch(d), own, :] = block
            fresh_kv[step, 0, at_batch(d)] = block
        if step == 0:
            loads[2].wait()
        values = jnp.dot(normed, wv_v[...], preferred_element_type=F32).astype(BF16)
        for d in range(n_batch):
            block = values[d * tok : (d + 1) * tok]
            v_all[step, 0, at_batch(d), own, :] = block
            fresh_kv[step, 1, at_batch(d)] = block
        next_waits = []
        if step < STEPS - 1:
            next_waits = send_kv(step + 1, fresh_kv.at[step, 0], fresh_kv.at[step, 1])
        else:
            out_k[...] = fresh_kv[step, 0]
            out_v[...] = fresh_kv[step, 1]
        if step == 0:
            loads[3].wait()
        queries = jnp.dot(normed, wq_v[...], preferred_element_type=F32).astype(BF16)

        scaled = queries.astype(F32) * HEAD ** (-0.5)
        wide_q = []
        for d in range(n_batch):
            block = jnp.broadcast_to(scaled[d * tok : (d + 1) * tok][None], (heads, tok, local))
            wide_q.append(jnp.where(head_mask, block, 0.0).astype(BF16).reshape(heads * tok, local))
        if step == 0:
            loads[4].wait()
            loads[5].wait()
        nt = (((1,), (1,)), ((), ()))
        text_scores = lax.dot_general(
            jnp.concatenate(wide_q, axis=0), tk_v[...], nt, preferred_element_type=F32
        )
        for copy in kv_waits:
            copy.wait()
        kv_waits = next_waits
        attended = []
        span = heads * tok
        for d in range(n_batch):
            s_img = lax.dot_general(
                wide_q[d], k_all[step, 0, at_batch(d)], nt, preferred_element_type=F32
            )
            s_txt = text_scores[d * span : (d + 1) * span]
            top = jnp.maximum(
                jnp.max(s_img, axis=1, keepdims=True), jnp.max(s_txt, axis=1, keepdims=True)
            )
            e_img = jnp.exp(s_img - top)
            e_txt = jnp.exp(s_txt - top)
            inv = 1.0 / (jnp.sum(e_img, axis=1, keepdims=True) + jnp.sum(e_txt, axis=1, keepdims=True))
            full = jnp.dot(
                (e_img * inv).astype(BF16), v_all[step, 0, at_batch(d)], preferred_element_type=F32
            ) + jnp.dot((e_txt * inv).astype(BF16), tv_v[...], preferred_element_type=F32)
            full = jnp.where(head_mask, full.reshape(heads, tok, local), 0.0)
            attended.append(jnp.sum(full, axis=0))
        rows_all = jnp.concatenate(attended, axis=0).astype(BF16)

        if step == 0:
            loads[6].wait()
        partial = jnp.dot(rows_all, wo_v[...], preferred_element_type=F32).astype(BF16)
        for d in range(1, n_batch):
            mix_send[step, d] = partial[d * tok : (d + 1) * tok]
        mix_send[step, 0] = partial[:tok]
        mix_all[step, 2 * batch + half] = partial[:tok]
        mix_waits = []
        for db, dc in reversed(others_bc):
            copy = pltpu.make_async_remote_copy(
                src_ref=mix_send.at[step, db],
                dst_ref=mix_all.at[step, 2 * batch + half],
                send_sem=mix_send_sem.at[step, db, dc],
                recv_sem=mix_recv_sem.at[step, db, dc],
                device_id=peer(patch, at_half(dc), at_batch(db)),
                device_id_type=MESH,
            )
            copy.start()
            mix_waits.append(copy)
        for copy in mix_waits:
            copy.wait()
        cond = mix_all[step, 0].astype(F32)
        uncond = mix_all[step, 1].astype(F32)
        for b in range(1, n_batch):
            cond = cond + mix_all[step, 2 * b].astype(F32)
            uncond = uncond + mix_all[step, 2 * b + 1].astype(F32)
        guess = state + uncond + guide_weight * (cond - uncond)
        keep = jnp.sqrt(abar[step + 1] / abar[step])
        push = jnp.sqrt(1.0 - abar[step + 1]) - keep * jnp.sqrt(1.0 - abar[step])
        state = keep * state + push * guess
    out_state[0] = state


def body(
    n_patch, n_batch, latent, stale_keys, stale_values, text_keys, text_values,
    w_query, w_key, w_value, w_out, norm_gain, norm_bias, timesteps,
):
    _, tok, width = latent.shape
    images = stale_keys.shape[0]
    local = w_query.shape[1]
    ctx = text_keys.shape[1]
    any_spec = pl.BlockSpec(memory_space=pl.ANY)
    vmem = pl.BlockSpec(memory_space=pltpu.VMEM)
    dma = pltpu.SemaphoreType.DMA
    return pl.pallas_call(
        functools.partial(kernel, n_patch, n_batch),
        out_shape=(
            jax.ShapeDtypeStruct(latent.shape, F32),
            jax.ShapeDtypeStruct(stale_keys.shape, BF16),
            jax.ShapeDtypeStruct(stale_values.shape, BF16),
        ),
        in_specs=[any_spec] * 9 + [vmem] * 2 + [pl.BlockSpec(memory_space=pltpu.SMEM)],
        out_specs=(vmem, vmem, vmem),
        scratch_shapes=[
            pltpu.VMEM((tok, width), F32),
            pltpu.VMEM((ctx, local), BF16),
            pltpu.VMEM((ctx, local), BF16),
            pltpu.VMEM((width, local), BF16),
            pltpu.VMEM((width, local), BF16),
            pltpu.VMEM((width, local), BF16),
            pltpu.VMEM((local, width), BF16),
            pltpu.VMEM((STEPS, 1, images, n_patch * tok, local), BF16),
            pltpu.VMEM((STEPS, 1, images, n_patch * tok, local), BF16),
            pltpu.VMEM((STEPS, 2, images, tok, local), BF16),
            pltpu.VMEM((STEPS, tok, width), BF16),
            pltpu.VMEM((STEPS, n_batch, tok, width), BF16),
            pltpu.VMEM((STEPS, 1, width), F32),
            pltpu.VMEM((STEPS, n_batch, 1, width), F32),
            pltpu.VMEM((STEPS, 8, LANES), F32),
            pltpu.VMEM((STEPS, n_batch, n_patch, 8, LANES), F32),
            pltpu.VMEM((STEPS, n_batch, tok, width), BF16),
            pltpu.VMEM((STEPS, 2 * n_batch, tok, width), BF16),
            dma((7,)),
            dma((STEPS, 2, n_patch)),
            dma((STEPS, 2, n_patch)),
            dma((STEPS, 2, n_batch)),
            dma((STEPS, 2, n_batch)),
            dma((STEPS, n_batch, n_patch)),
            dma((STEPS, n_batch, n_patch)),
            dma((STEPS, n_batch, 2)),
            dma((STEPS, n_batch, 2)),
        ],
        compiler_params=pltpu.CompilerParams(
            collective_id=0, has_side_effects=True, vmem_limit_bytes=40 * 1024 * 1024
        ),
    )(
        latent, stale_keys, stale_values, text_keys, text_values, w_query, w_key, w_value, w_out,
        norm_gain.reshape(1, width), norm_bias.reshape(1, width), timesteps.reshape(1, -1),
    )


def solution(mesh):
    return jax.shard_map(
        functools.partial(body, mesh.shape["patch"], mesh.shape["batch"]),
        mesh=mesh,
        in_specs=(
            P(("prompts", "batch"), "patch", None),
            P("prompts", "patch", "batch"),
            P("prompts", "patch", "batch"),
            P(("prompts", "cfg"), None, "batch"),
            P(("prompts", "cfg"), None, "batch"),
            P(None, "batch"),
            P(None, "batch"),
            P(None, "batch"),
            P("batch", None),
            P(),
            P(),
            P("prompts"),
        ),
        out_specs=(
            P(("prompts", "batch"), "patch", None),
            P("prompts", "patch", "batch"),
            P("prompts", "patch", "batch"),
        ),
        check_vma=False,
    )
```

```python
import functools
import math

import jax
import jax.numpy as jnp
from jax import lax
from jax.experimental import pallas as pl
from jax.experimental.pallas import tpu as pltpu
from jax.sharding import PartitionSpec as P

HEAD = 64
GROUPS = 32
STEPS = 2
LANES = 128

guide_weight = 5.0
norm_eps = 1e-06
MESH = pl.DeviceIdType.MESH
F32 = jnp.float32
BF16 = jnp.bfloat16


def split3(x):
    hi = x.astype(BF16)
    rest = x - hi.astype(F32)
    mid = rest.astype(BF16)
    low = (rest - mid.astype(F32)).astype(BF16)
    return hi, mid, low


def exact_dot(x, onehot, contract):
    rows = x.shape[0]
    parts = jnp.concatenate([p.astype(F32) for p in split3(x)], axis=0).astype(BF16)
    out = lax.dot_general(parts, onehot, (((1,), (contract,)), ((), ())), preferred_element_type=F32)
    return out[:rows] + out[rows : 2 * rows] + out[2 * rows :]


def kernel(
    n_patch,
    n_batch,
    latent,
    stale_k,
    stale_v,
    text_k,
    text_v,
    w_query,
    w_key,
    w_value,
    w_out,
    gain,
    bias,
    timesteps,
    out_state,
    out_k,
    out_v,
    state_v,
    tk_v,
    tv_v,
    wq_v,
    wk_v,
    wv_v,
    wo_v,
    kv_all,
    stale_kv,
    fresh_kv,
    dev_send,
    dev_recv,
    cen_send,
    cen_recv,
    stat_send,
    stat_all,
    mix_send,
    mix_all,
    load_sem,
    kv_send_sem,
    kv_recv_sem,
    hand_send_sem,
    hand_recv_sem,
    dev_send_sem,
    dev_recv_sem,
    stat_send_sem,
    stat_recv_sem,
    mix_send_sem,
    mix_recv_sem,
):
    patch = lax.axis_index("patch")
    half = lax.axis_index("cfg")
    batch = lax.axis_index("batch")
    tok = state_v.shape[0]
    width = state_v.shape[1]
    images = kv_all.shape[2]
    local = wq_v.shape[1]
    heads = local // HEAD
    group_width = width // GROUPS
    count = float(tok * n_patch * group_width)

    loads = [
        pltpu.make_async_copy(src, dst, load_sem.at[i])
        for i, (src, dst) in enumerate(
            [
                (latent.at[0], state_v),
                (stale_k, stale_kv.at[0]),
                (stale_v, stale_kv.at[1]),
                (w_key, wk_v),
                (w_value, wv_v),
                (w_query, wq_v),
                (text_k.at[0], tk_v),
                (text_v.at[0], tv_v),
                (w_out, wo_v),
            ]
        )
    ]
    for copy in loads:
        copy.start()

    def peer(p, c, b):
        return {"patch": p, "cfg": c, "batch": b}

    others_pb = [(dp, db) for db in range(n_batch) for dp in range(n_patch) if (dp, db) != (0, 0)]
    others_bc = [(db, dc) for db in range(n_batch) for dc in range(2) if (db, dc) != (0, 0)]

    def at_patch(d):
        return lax.rem(patch + d, n_patch) if d else patch

    def at_batch(d):
        return lax.rem(batch + d, n_batch) if d else batch

    def at_half(d):
        return lax.rem(half + d, 2) if d else half

    barrier = pltpu.get_barrier_semaphore()
    greeted = 0
    for dp, db in others_pb:
        pl.semaphore_signal(barrier, inc=1, device_id=peer(at_patch(dp), half, at_batch(db)), device_id_type=MESH)
        greeted += 1
    for db, dc in others_bc:
        if dc:
            pl.semaphore_signal(barrier, inc=1, device_id=peer(patch, at_half(dc), at_batch(db)), device_id_type=MESH)
            greeted += 1

    chan = lax.broadcasted_iota(jnp.int32, (width, LANES), 0)
    lane = lax.broadcasted_iota(jnp.int32, (width, LANES), 1)
    low = lane * group_width
    onehot = jnp.where((chan >= low) & (chan < low + group_width), 1.0, 0.0).astype(BF16)

    head_id = lax.broadcasted_iota(jnp.int32, (heads, tok, local), 0) * HEAD
    col_id = lax.broadcasted_iota(jnp.int32, (heads, tok, local), 2)
    head_mask = (col_id >= head_id) & (col_id < head_id + HEAD)

    sub = lax.broadcasted_iota(jnp.int32, (8, LANES), 0)
    lan = lax.broadcasted_iota(jnp.int32, (8, LANES), 1)
    grid = sub * LANES + lan
    ramp = grid.astype(F32) / 999.0
    root = math.sqrt(0.00085) + ramp * (math.sqrt(0.012) - math.sqrt(0.00085))
    logs = jnp.log1p(-root * root)

    def alpha_bar(t):
        picked = jnp.where((grid <= t) & (grid < 1000), logs, 0.0)
        return jnp.exp(jnp.sum(jnp.sum(picked, axis=1, keepdims=True), axis=0, keepdims=True))

    abar = [alpha_bar(timesteps[s]) for s in range(STEPS + 1)]

    def slot(step, which, p):
        return kv_all.at[step, which, :, pl.ds(pl.multiple_of(p * tok, tok), tok), :]

    def send_kv(step, src):
        made = []
        for d in range(1, n_patch):
            copy = pltpu.make_async_remote_copy(
                src_ref=src.at[half],
                dst_ref=slot(step, half, patch),
                send_sem=kv_send_sem.at[step, d],
                recv_sem=kv_recv_sem.at[step, d],
                device_id=peer(at_patch(d), half, batch),
                device_id_type=MESH,
            )
            copy.start()
            made.append(copy)
        return made

    def hand_over(step, arriving):
        made = []
        for d, copy in enumerate(arriving, 1):
            copy.wait()
            here = slot(step, half, at_patch(n_patch - d))
            copy = pltpu.make_async_remote_copy(
                src_ref=here,
                dst_ref=here,
                send_sem=hand_send_sem.at[step, d],
                recv_sem=hand_recv_sem.at[step, d],
                device_id=peer(patch, at_half(1), batch),
                device_id_type=MESH,
            )
            copy.start()
            made.append(copy)
        return made

    loads[0].wait()
    state = state_v[...]
    gain_row = gain[...].reshape(1, width)
    bias_row = bias[...].reshape(1, width)

    for step in range(STEPS):
        col_sum = jnp.sum(state, axis=0, keepdims=True)
        col_sq = jnp.sum(state * state, axis=0, keepdims=True)
        centre = col_sum / float(tok)
        cen_send[step] = centre
        dev_send[step] = (state - centre).astype(BF16)
        if step == 0:
            pl.semaphore_wait(barrier, greeted)
        dev_waits = []
        for d in range(1, n_batch):
            for j, (src, dst) in enumerate([(dev_send, dev_recv), (cen_send, cen_recv)]):
                copy = pltpu.make_async_remote_copy(
                    src_ref=src.at[step],
                    dst_ref=dst.at[step, d],
                    send_sem=dev_send_sem.at[step, j, d],
                    recv_sem=dev_recv_sem.at[step, j, d],
                    device_id=peer(patch, half, at_batch(d)),
                    device_id_type=MESH,
                )
                copy.start()
                dev_waits.append(copy)
        pad = jnp.zeros((6, width), F32)
        compact = exact_dot(jnp.concatenate([col_sum, col_sq, pad], axis=0), onehot, 0)
        stat_send[step] = compact
        stat_all[step, batch, patch] = compact
        stat_waits = []
        for dp, db in others_pb:
            copy = pltpu.make_async_remote_copy(
                src_ref=stat_send.at[step],
                dst_ref=stat_all.at[step, batch, patch],
                send_sem=stat_send_sem.at[step, db, dp],
                recv_sem=stat_recv_sem.at[step, db, dp],
                device_id=peer(at_patch(dp), half, at_batch(db)),
                device_id_type=MESH,
            )
            copy.start()
            stat_waits.append(copy)
        if step == 0:
            loads[1].wait()
            loads[2].wait()
            arriving = send_kv(0, stale_kv)
        else:
            handed = hand_over(step, arriving)
        for copy in stat_waits:
            copy.wait()

        rows = []
        for d in range(n_batch):
            total = stat_all[step, at_batch(d), 0]
            for p in range(1, n_patch):
                total = total + stat_all[step, at_batch(d), p]
            total = total / count
            mean = total[0:1]
            scale = lax.rsqrt(total[1:2] - mean * mean + norm_eps)
            rows += [mean, scale]
        pad_rows = -len(rows) % 8
        if pad_rows:
            rows.append(jnp.zeros((pad_rows, LANES), F32))
        wide = exact_dot(jnp.concatenate(rows, axis=0), onehot, 1)
        for copy in dev_waits:
            copy.wait()
        pieces = []
        for d in range(n_batch):
            mean = wide[2 * d : 2 * d + 1]
            scale = wide[2 * d + 1 : 2 * d + 2]
            if d == 0:
                shifted = state - mean
            else:
                shifted = dev_recv[step, n_batch - d].astype(F32) + (cen_recv[step, n_batch - d] - mean)
            pieces.append((shifted * scale * gain_row + bias_row).astype(BF16))
        normed = jnp.concatenate(pieces, axis=0)

        own = pl.ds(pl.multiple_of(patch * tok, tok), tok)
        if step == 0:
            loads[3].wait()
        keys = jnp.dot(normed, wk_v[...], preferred_element_type=F32).astype(BF16)
        for d in range(n_batch):
            block = keys[d * tok : (d + 1) * tok]
            kv_all[step, 0, at_batch(d), own, :] = block
            fresh_kv[step, 0, at_batch(d)] = block
        if step == 0:
            loads[4].wait()
        values = jnp.dot(normed, wv_v[...], preferred_element_type=F32).astype(BF16)
        for d in range(n_batch):
            block = values[d * tok : (d + 1) * tok]
            kv_all[step, 1, at_batch(d), own, :] = block
            fresh_kv[step, 1, at_batch(d)] = block
        if step == STEPS - 1:
            out_k[...] = fresh_kv[step, 0]
            out_v[...] = fresh_kv[step, 1]
        if step == 0:
            loads[5].wait()
        queries = jnp.dot(normed, wq_v[...], preferred_element_type=F32).astype(BF16)

        scaled = queries.astype(F32) * HEAD ** (-0.5)
        wide_q = []
        for d in range(n_batch):
            block = jnp.broadcast_to(scaled[d * tok : (d + 1) * tok][None], (heads, tok, local))
            wide_q.append(jnp.where(head_mask, block, 0.0).astype(BF16).reshape(heads * tok, local))
        if step == 0:
            loads[6].wait()
            loads[7].wait()
        nt = (((1,), (1,)), ((), ()))
        text_scores = lax.dot_general(
            jnp.concatenate(wide_q, axis=0), tk_v[...], nt, preferred_element_type=F32
        )
        if step == 0:
            handed = hand_over(step, arriving)
        if step < STEPS - 1:
            arriving = send_kv(step + 1, fresh_kv.at[step])
        for copy in handed:
            copy.wait()
        attended = []
        span = heads * tok
        for d in range(n_batch):
            s_img = lax.dot_general(
                wide_q[d], kv_all[step, 0, at_batch(d)], nt, preferred_element_type=F32
            )
            s_txt = text_scores[d * span : (d + 1) * span]
            top = jnp.maximum(
                jnp.max(s_img, axis=1, keepdims=True), jnp.max(s_txt, axis=1, keepdims=True)
            )
            e_img = jnp.exp(s_img - top)
            e_txt = jnp.exp(s_txt - top)
            inv = 1.0 / (jnp.sum(e_img, axis=1, keepdims=True) + jnp.sum(e_txt, axis=1, keepdims=True))
            full = jnp.dot(
                (e_img * inv).astype(BF16), kv_all[step, 1, at_batch(d)], preferred_element_type=F32
            ) + jnp.dot((e_txt * inv).astype(BF16), tv_v[...], preferred_element_type=F32)
            full = jnp.where(head_mask, full.reshape(heads, tok, local), 0.0)
            attended.append(jnp.sum(full, axis=0))
        rows_all = jnp.concatenate(attended, axis=0).astype(BF16)

        if step == 0:
            loads[8].wait()
        partial = jnp.dot(rows_all, wo_v[...], preferred_element_type=F32).astype(BF16)
        for d in range(1, n_batch):
            mix_send[step, d] = partial[d * tok : (d + 1) * tok]
        mix_send[step, 0] = partial[:tok]
        mix_all[step, 2 * batch + half] = partial[:tok]
        mix_waits = []
        for db, dc in reversed(others_bc):
            copy = pltpu.make_async_remote_copy(
                src_ref=mix_send.at[step, db],
                dst_ref=mix_all.at[step, 2 * batch + half],
                send_sem=mix_send_sem.at[step, db, dc],
                recv_sem=mix_recv_sem.at[step, db, dc],
                device_id=peer(patch, at_half(dc), at_batch(db)),
                device_id_type=MESH,
            )
            copy.start()
            mix_waits.append(copy)
        for copy in mix_waits:
            copy.wait()
        cond = mix_all[step, 0].astype(F32)
        uncond = mix_all[step, 1].astype(F32)
        for b in range(1, n_batch):
            cond = cond + mix_all[step, 2 * b].astype(F32)
            uncond = uncond + mix_all[step, 2 * b + 1].astype(F32)
        guess = state + uncond + guide_weight * (cond - uncond)
        keep = jnp.sqrt(abar[step + 1] / abar[step])
        push = jnp.sqrt(1.0 - abar[step + 1]) - keep * jnp.sqrt(1.0 - abar[step])
        state = keep * state + push * guess
    out_state[0] = state


def body(
    n_patch, n_batch, latent, stale_keys, stale_values, text_keys, text_values,
    w_query, w_key, w_value, w_out, norm_gain, norm_bias, timesteps,
):
    _, tok, width = latent.shape
    images = stale_keys.shape[0]
    local = w_query.shape[1]
    ctx = text_keys.shape[1]
    any_spec = pl.BlockSpec(memory_space=pl.ANY)
    vmem = pl.BlockSpec(memory_space=pltpu.VMEM)
    dma = pltpu.SemaphoreType.DMA
    return pl.pallas_call(
        functools.partial(kernel, n_patch, n_batch),
        out_shape=(
            jax.ShapeDtypeStruct(latent.shape, F32),
            jax.ShapeDtypeStruct(stale_keys.shape, BF16),
            jax.ShapeDtypeStruct(stale_values.shape, BF16),
        ),
        in_specs=[any_spec] * 9 + [vmem] * 2 + [pl.BlockSpec(memory_space=pltpu.SMEM)],
        out_specs=(vmem, vmem, vmem),
        scratch_shapes=[
            pltpu.VMEM((tok, width), F32),
            pltpu.VMEM((ctx, local), BF16),
            pltpu.VMEM((ctx, local), BF16),
            pltpu.VMEM((width, local), BF16),
            pltpu.VMEM((width, local), BF16),
            pltpu.VMEM((width, local), BF16),
            pltpu.VMEM((local, width), BF16),
            pltpu.VMEM((STEPS, 2, images, n_patch * tok, local), BF16),
            pltpu.VMEM((2, images, tok, local), BF16),
            pltpu.VMEM((STEPS, 2, images, tok, local), BF16),
            pltpu.VMEM((STEPS, tok, width), BF16),
            pltpu.VMEM((STEPS, n_batch, tok, width), BF16),
            pltpu.VMEM((STEPS, 1, width), F32),
            pltpu.VMEM((STEPS, n_batch, 1, width), F32),
            pltpu.VMEM((STEPS, 8, LANES), F32),
            pltpu.VMEM((STEPS, n_batch, n_patch, 8, LANES), F32),
            pltpu.VMEM((STEPS, n_batch, tok, width), BF16),
            pltpu.VMEM((STEPS, 2 * n_batch, tok, width), BF16),
            dma((9,)),
            dma((STEPS, n_patch)),
            dma((STEPS, n_patch)),
            dma((STEPS, n_patch)),
            dma((STEPS, n_patch)),
            dma((STEPS, 2, n_batch)),
            dma((STEPS, 2, n_batch)),
            dma((STEPS, n_batch, n_patch)),
            dma((STEPS, n_batch, n_patch)),
            dma((STEPS, n_batch, 2)),
            dma((STEPS, n_batch, 2)),
        ],
        compiler_params=pltpu.CompilerParams(
            collective_id=0, has_side_effects=True, vmem_limit_bytes=63 * 1024 * 1024
        ),
    )(
        latent, stale_keys, stale_values, text_keys, text_values, w_query, w_key, w_value, w_out,
        norm_gain, norm_bias, timesteps,
    )


def solution(mesh):
    return jax.shard_map(
        functools.partial(body, mesh.shape["patch"], mesh.shape["batch"]),
        mesh=mesh,
        in_specs=(
            P(("prompts", "batch"), "patch", None),
            P("prompts", "patch", "batch"),
            P("prompts", "patch", "batch"),
            P(("prompts", "cfg"), None, "batch"),
            P(("prompts", "cfg"), None, "batch"),
            P(None, "batch"),
            P(None, "batch"),
            P(None, "batch"),
            P("batch", None),
            P(),
            P(),
            P("prompts"),
        ),
        out_specs=(
            P(("prompts", "batch"), "patch", None),
            P("prompts", "patch", "batch"),
            P("prompts", "patch", "batch"),
        ),
        check_vma=False,
    )
```

```python
import functools
import math

import jax
import jax.numpy as jnp
from jax import lax
from jax.experimental import pallas as pl
from jax.experimental.pallas import tpu as pltpu
from jax.sharding import PartitionSpec as P

HEAD = 64
GROUPS = 32
STEPS = 2
LANES = 128

guide_weight = 5.0
norm_eps = 1e-06
MESH = pl.DeviceIdType.MESH
F32 = jnp.float32
BF16 = jnp.bfloat16


def split3(x):
    hi = x.astype(BF16)
    rest = x - hi.astype(F32)
    mid = rest.astype(BF16)
    low = (rest - mid.astype(F32)).astype(BF16)
    return hi, mid, low


def exact_dot(x, onehot, contract):
    rows = x.shape[0]
    parts = jnp.concatenate([p.astype(F32) for p in split3(x)], axis=0).astype(BF16)
    out = lax.dot_general(parts, onehot, (((1,), (contract,)), ((), ())), preferred_element_type=F32)
    return out[:rows] + out[rows : 2 * rows] + out[2 * rows :]


def kernel(
    n_patch,
    n_batch,
    latent,
    stale_k,
    stale_v,
    text_k,
    text_v,
    w_query,
    w_key,
    w_value,
    w_out,
    gain,
    bias,
    timesteps,
    out_state,
    out_k,
    out_v,
    state_v,
    gain_v,
    bias_v,
    tk_v,
    tv_v,
    wq_v,
    wk_v,
    wv_v,
    wo_v,
    kv_all,
    stale_kv,
    fresh_kv,
    dev_send,
    dev_recv,
    cen_send,
    cen_recv,
    stat_send,
    stat_all,
    mix_send,
    mix_all,
    load_sem,
    kv_send_sem,
    kv_recv_sem,
    hand_send_sem,
    hand_recv_sem,
    dev_send_sem,
    dev_recv_sem,
    stat_send_sem,
    stat_recv_sem,
    mix_send_sem,
    mix_recv_sem,
):
    patch = lax.axis_index("patch")
    half = lax.axis_index("cfg")
    batch = lax.axis_index("batch")
    tok = state_v.shape[0]
    width = state_v.shape[1]
    images = kv_all.shape[2]
    local = wq_v.shape[1]
    heads = local // HEAD
    group_width = width // GROUPS
    count = float(tok * n_patch * group_width)

    loads = [
        pltpu.make_async_copy(src, dst, load_sem.at[i])
        for i, (src, dst) in enumerate(
            [
                (latent.at[0], state_v),
                (stale_k, stale_kv.at[0]),
                (stale_v, stale_kv.at[1]),
                (w_key, wk_v),
                (w_value, wv_v),
                (w_query, wq_v),
                (text_k.at[0], tk_v),
                (text_v.at[0], tv_v),
                (w_out, wo_v),
                (gain, gain_v),
                (bias, bias_v),
            ]
        )
    ]
    for copy in loads:
        copy.start()

    def peer(p, c, b):
        return {"patch": p, "cfg": c, "batch": b}

    others_pb = [(dp, db) for db in range(n_batch) for dp in range(n_patch) if (dp, db) != (0, 0)]
    others_bc = [(db, dc) for db in range(n_batch) for dc in range(2) if (db, dc) != (0, 0)]

    def at_patch(d):
        return lax.rem(patch + d, n_patch) if d else patch

    def at_batch(d):
        return lax.rem(batch + d, n_batch) if d else batch

    def at_half(d):
        return lax.rem(half + d, 2) if d else half

    barrier = pltpu.get_barrier_semaphore()
    greeted = 0
    for dp, db in others_pb:
        pl.semaphore_signal(barrier, inc=1, device_id=peer(at_patch(dp), half, at_batch(db)), device_id_type=MESH)
        greeted += 1
    for db, dc in others_bc:
        if dc:
            pl.semaphore_signal(barrier, inc=1, device_id=peer(patch, at_half(dc), at_batch(db)), device_id_type=MESH)
            greeted += 1

    chan = lax.broadcasted_iota(jnp.int32, (width, LANES), 0)
    lane = lax.broadcasted_iota(jnp.int32, (width, LANES), 1)
    low = lane * group_width
    onehot = jnp.where((chan >= low) & (chan < low + group_width), 1.0, 0.0).astype(BF16)

    head_id = lax.broadcasted_iota(jnp.int32, (heads, tok, local), 0) * HEAD
    col_id = lax.broadcasted_iota(jnp.int32, (heads, tok, local), 2)
    head_mask = (col_id >= head_id) & (col_id < head_id + HEAD)

    sub = lax.broadcasted_iota(jnp.int32, (8, LANES), 0)
    lan = lax.broadcasted_iota(jnp.int32, (8, LANES), 1)
    grid = sub * LANES + lan
    ramp = grid.astype(F32) / 999.0
    root = math.sqrt(0.00085) + ramp * (math.sqrt(0.012) - math.sqrt(0.00085))
    logs = jnp.log1p(-root * root)

    def alpha_bar(t):
        picked = jnp.where((grid <= t) & (grid < 1000), logs, 0.0)
        return jnp.exp(jnp.sum(jnp.sum(picked, axis=1, keepdims=True), axis=0, keepdims=True))

    abar = [alpha_bar(timesteps[s]) for s in range(STEPS + 1)]

    def slot(step, which, p):
        return kv_all.at[step, which, :, pl.ds(pl.multiple_of(p * tok, tok), tok), :]

    def send_kv(step, src):
        made = []
        for d in range(1, n_patch):
            copy = pltpu.make_async_remote_copy(
                src_ref=src.at[half],
                dst_ref=slot(step, half, patch),
                send_sem=kv_send_sem.at[step, d],
                recv_sem=kv_recv_sem.at[step, d],
                device_id=peer(at_patch(d), half, batch),
                device_id_type=MESH,
            )
            copy.start()
            made.append(copy)
        return made

    def hand_over(step, arriving):
        made = []
        for d, copy in enumerate(arriving, 1):
            copy.wait()
            here = slot(step, half, at_patch(n_patch - d))
            copy = pltpu.make_async_remote_copy(
                src_ref=here,
                dst_ref=here,
                send_sem=hand_send_sem.at[step, d],
                recv_sem=hand_recv_sem.at[step, d],
                device_id=peer(patch, at_half(1), batch),
                device_id_type=MESH,
            )
            copy.start()
            made.append(copy)
        return made

    loads[0].wait()
    state = state_v[...]

    for step in range(STEPS):
        col_sum = jnp.sum(state, axis=0, keepdims=True)
        col_sq = jnp.sum(state * state, axis=0, keepdims=True)
        centre = col_sum / float(tok)
        cen_send[step] = centre
        dev_send[step] = (state - centre).astype(BF16)
        if step == 0:
            pl.semaphore_wait(barrier, greeted)
        dev_waits = []
        for d in range(1, n_batch):
            for j, (src, dst) in enumerate([(dev_send, dev_recv), (cen_send, cen_recv)]):
                copy = pltpu.make_async_remote_copy(
                    src_ref=src.at[step],
                    dst_ref=dst.at[step, d],
                    send_sem=dev_send_sem.at[step, j, d],
                    recv_sem=dev_recv_sem.at[step, j, d],
                    device_id=peer(patch, half, at_batch(d)),
                    device_id_type=MESH,
                )
                copy.start()
                dev_waits.append(copy)
        pad = jnp.zeros((6, width), F32)
        compact = exact_dot(jnp.concatenate([col_sum, col_sq, pad], axis=0), onehot, 0)
        stat_send[step] = compact
        stat_all[step, batch, patch] = compact
        stat_waits = []
        for dp, db in others_pb:
            copy = pltpu.make_async_remote_copy(
                src_ref=stat_send.at[step],
                dst_ref=stat_all.at[step, batch, patch],
                send_sem=stat_send_sem.at[step, db, dp],
                recv_sem=stat_recv_sem.at[step, db, dp],
                device_id=peer(at_patch(dp), half, at_batch(db)),
                device_id_type=MESH,
            )
            copy.start()
            stat_waits.append(copy)
        if step == 0:
            loads[1].wait()
            loads[2].wait()
            arriving = send_kv(0, stale_kv)
        else:
            handed = hand_over(step, arriving)
        for copy in stat_waits:
            copy.wait()

        rows = []
        for d in range(n_batch):
            total = stat_all[step, at_batch(d), 0]
            for p in range(1, n_patch):
                total = total + stat_all[step, at_batch(d), p]
            total = total / count
            mean = total[0:1]
            scale = lax.rsqrt(total[1:2] - mean * mean + norm_eps)
            rows += [mean, scale]
        pad_rows = -len(rows) % 8
        if pad_rows:
            rows.append(jnp.zeros((pad_rows, LANES), F32))
        wide = exact_dot(jnp.concatenate(rows, axis=0), onehot, 1)
        for copy in dev_waits:
            copy.wait()
        if step == 0:
            loads[9].wait()
            loads[10].wait()
            gain_row = gain_v[...].reshape(1, width)
            bias_row = bias_v[...].reshape(1, width)
        pieces = []
        for d in range(n_batch):
            mean = wide[2 * d : 2 * d + 1]
            scale = wide[2 * d + 1 : 2 * d + 2]
            if d == 0:
                shifted = state - mean
            else:
                shifted = dev_recv[step, n_batch - d].astype(F32) + (cen_recv[step, n_batch - d] - mean)
            pieces.append((shifted * scale * gain_row + bias_row).astype(BF16))
        normed = jnp.concatenate(pieces, axis=0)

        own = pl.ds(pl.multiple_of(patch * tok, tok), tok)
        if step == 0:
            loads[3].wait()
        keys = jnp.dot(normed, wk_v[...], preferred_element_type=F32).astype(BF16)
        for d in range(n_batch):
            block = keys[d * tok : (d + 1) * tok]
            kv_all[step, 0, at_batch(d), own, :] = block
            fresh_kv[step, 0, at_batch(d)] = block
        if step == 0:
            loads[4].wait()
        values = jnp.dot(normed, wv_v[...], preferred_element_type=F32).astype(BF16)
        for d in range(n_batch):
            block = values[d * tok : (d + 1) * tok]
            kv_all[step, 1, at_batch(d), own, :] = block
            fresh_kv[step, 1, at_batch(d)] = block
        if step == STEPS - 1:
            out_k[...] = fresh_kv[step, 0]
            out_v[...] = fresh_kv[step, 1]
        if step == 0:
            loads[5].wait()
        queries = jnp.dot(normed, wq_v[...], preferred_element_type=F32).astype(BF16)

        scaled = queries.astype(F32) * HEAD ** (-0.5)
        wide_q = []
        for d in range(n_batch):
            block = jnp.broadcast_to(scaled[d * tok : (d + 1) * tok][None], (heads, tok, local))
            wide_q.append(jnp.where(head_mask, block, 0.0).astype(BF16).reshape(heads * tok, local))
        if step == 0:
            loads[6].wait()
            loads[7].wait()
        nt = (((1,), (1,)), ((), ()))
        text_scores = lax.dot_general(
            jnp.concatenate(wide_q, axis=0), tk_v[...], nt, preferred_element_type=F32
        )
        if step == 0:
            handed = hand_over(step, arriving)
        if step < STEPS - 1:
            arriving = send_kv(step + 1, fresh_kv.at[step])
        for copy in handed:
            copy.wait()
        attended = []
        span = heads * tok
        for d in range(n_batch):
            s_img = lax.dot_general(
                wide_q[d], kv_all[step, 0, at_batch(d)], nt, preferred_element_type=F32
            )
            s_txt = text_scores[d * span : (d + 1) * span]
            top = jnp.maximum(
                jnp.max(s_img, axis=1, keepdims=True), jnp.max(s_txt, axis=1, keepdims=True)
            )
            e_img = jnp.exp(s_img - top)
            e_txt = jnp.exp(s_txt - top)
            inv = 1.0 / (jnp.sum(e_img, axis=1, keepdims=True) + jnp.sum(e_txt, axis=1, keepdims=True))
            full = jnp.dot(
                (e_img * inv).astype(BF16), kv_all[step, 1, at_batch(d)], preferred_element_type=F32
            ) + jnp.dot((e_txt * inv).astype(BF16), tv_v[...], preferred_element_type=F32)
            full = jnp.where(head_mask, full.reshape(heads, tok, local), 0.0)
            attended.append(jnp.sum(full, axis=0))
        rows_all = jnp.concatenate(attended, axis=0).astype(BF16)

        if step == 0:
            loads[8].wait()
        partial = jnp.dot(rows_all, wo_v[...], preferred_element_type=F32).astype(BF16)
        for d in range(1, n_batch):
            mix_send[step, d] = partial[d * tok : (d + 1) * tok]
        mix_send[step, 0] = partial[:tok]
        mix_all[step, 2 * batch + half] = partial[:tok]
        mix_waits = []
        for db, dc in reversed(others_bc):
            copy = pltpu.make_async_remote_copy(
                src_ref=mix_send.at[step, db],
                dst_ref=mix_all.at[step, 2 * batch + half],
                send_sem=mix_send_sem.at[step, db, dc],
                recv_sem=mix_recv_sem.at[step, db, dc],
                device_id=peer(patch, at_half(dc), at_batch(db)),
                device_id_type=MESH,
            )
            copy.start()
            mix_waits.append(copy)
        for copy in mix_waits:
            copy.wait()
        cond = mix_all[step, 0].astype(F32)
        uncond = mix_all[step, 1].astype(F32)
        for b in range(1, n_batch):
            cond = cond + mix_all[step, 2 * b].astype(F32)
            uncond = uncond + mix_all[step, 2 * b + 1].astype(F32)
        guess = state + uncond + guide_weight * (cond - uncond)
        keep = jnp.sqrt(abar[step + 1] / abar[step])
        push = jnp.sqrt(1.0 - abar[step + 1]) - keep * jnp.sqrt(1.0 - abar[step])
        state = keep * state + push * guess
    out_state[0] = state


def body(
    n_patch, n_batch, latent, stale_keys, stale_values, text_keys, text_values,
    w_query, w_key, w_value, w_out, norm_gain, norm_bias, timesteps,
):
    _, tok, width = latent.shape
    images = stale_keys.shape[0]
    local = w_query.shape[1]
    ctx = text_keys.shape[1]
    hbm = pl.BlockSpec(memory_space=pl.ANY)
    vmem = pl.BlockSpec(memory_space=pltpu.VMEM)
    dma = pltpu.SemaphoreType.DMA
    return pl.pallas_call(
        functools.partial(kernel, n_patch, n_batch),
        out_shape=(
            pltpu.VMEM(latent.shape, F32),
            pltpu.VMEM(stale_keys.shape, BF16),
            pltpu.VMEM(stale_values.shape, BF16),
        ),
        in_specs=[hbm] * 11 + [pl.BlockSpec(memory_space=pltpu.SMEM)],
        out_specs=(vmem, vmem, vmem),
        scratch_shapes=[
            pltpu.VMEM((tok, width), F32),
            pltpu.VMEM((width,), F32),
            pltpu.VMEM((width,), F32),
            pltpu.VMEM((ctx, local), BF16),
            pltpu.VMEM((ctx, local), BF16),
            pltpu.VMEM((width, local), BF16),
            pltpu.VMEM((width, local), BF16),
            pltpu.VMEM((width, local), BF16),
            pltpu.VMEM((local, width), BF16),
            pltpu.VMEM((STEPS, 2, images, n_patch * tok, local), BF16),
            pltpu.VMEM((2, images, tok, local), BF16),
            pltpu.VMEM((STEPS, 2, images, tok, local), BF16),
            pltpu.VMEM((STEPS, tok, width), BF16),
            pltpu.VMEM((STEPS, n_batch, tok, width), BF16),
            pltpu.VMEM((STEPS, 1, width), F32),
            pltpu.VMEM((STEPS, n_batch, 1, width), F32),
            pltpu.VMEM((STEPS, 8, LANES), F32),
            pltpu.VMEM((STEPS, n_batch, n_patch, 8, LANES), F32),
            pltpu.VMEM((STEPS, n_batch, tok, width), BF16),
            pltpu.VMEM((STEPS, 2 * n_batch, tok, width), BF16),
            dma((11,)),
            dma((STEPS, n_patch)),
            dma((STEPS, n_patch)),
            dma((STEPS, n_patch)),
            dma((STEPS, n_patch)),
            dma((STEPS, 2, n_batch)),
            dma((STEPS, 2, n_batch)),
            dma((STEPS, n_batch, n_patch)),
            dma((STEPS, n_batch, n_patch)),
            dma((STEPS, n_batch, 2)),
            dma((STEPS, n_batch, 2)),
        ],
        compiler_params=pltpu.CompilerParams(
            collective_id=0, has_side_effects=True, vmem_limit_bytes=62 * 1024 * 1024
        ),
    )(
        latent, stale_keys, stale_values, text_keys, text_values, w_query, w_key, w_value, w_out,
        norm_gain, norm_bias, timesteps,
    )


def solution(mesh):
    return jax.shard_map(
        functools.partial(body, mesh.shape["patch"], mesh.shape["batch"]),
        mesh=mesh,
        in_specs=(
            P(("prompts", "batch"), "patch", None),
            P("prompts", "patch", "batch"),
            P("prompts", "patch", "batch"),
            P(("prompts", "cfg"), None, "batch"),
            P(("prompts", "cfg"), None, "batch"),
            P(None, "batch"),
            P(None, "batch"),
            P(None, "batch"),
            P("batch", None),
            P(),
            P(),
            P("prompts"),
        ),
        out_specs=(
            P(("prompts", "batch"), "patch", None),
            P("prompts", "patch", "batch"),
            P("prompts", "patch", "batch"),
        ),
        check_vma=False,
    )
```
